32 devices in a mesh: groups: 2 (over y), expert: 4 (over z), dp: 2 (over x), head: 2 (over core).
Axes of the slice: x: 2, y: 2, z: 4, core: 2. Of those that a mesh axis runs over, the one named last changes fastest.
Arguments:
- hidden: bfloat16 [4, 1024, 1536], P(('groups', 'dp'), ('expert', 'head')), parts along dimension 0, may hold values from -6 to 6
- modulation: float32 [4, 3, 1536], P(('groups', 'dp')), parts along dimension 0, may hold values from -3 to 3
- router_weight: float32 [1536, 16], replicated, may hold values from -0.15625 to 0.15625
- route_ids: int32 [4, 1024, 2], P(('groups', 'dp'), ('expert', 'head')), parts along dimension 0, may hold values from 0 to 15, all different within a row; in each aligned block of 128 rows (0 to 127, 128 to 255, ..., all dimensions but the last counted through in order) at most 32 rows name the same one
- gate_weight: bfloat16 [1536, 98304], P(None, ('expert', 'dp', 'head')), may hold values from -0.15625 to 0.15625
- up_weight: bfloat16 [1536, 98304], P(None, ('expert', 'dp', 'head')), may hold values from -0.15625 to 0.15625
- down_weight: bfloat16 [98304, 1536], P(('expert', 'dp', 'head')), may hold values from -0.078125 to 0.078125
- main_final: bfloat16 [1536, 16], replicated, may hold values from -0.15625 to 0.15625
- guide_qkv: bfloat16 [4, 1024, 6, 192], P(('groups', 'dp'), 'expert', 'head'), parts along dimension 0, may hold values from -6 to 6
- guide_out: bfloat16 [6, 64, 384], P('head'), may hold values from -0.3125 to 0.3125
- guide_final: bfloat16 [384, 16], replicated, may hold values from -0.3125 to 0.3125
- latent: float32 [4, 1024, 16], P(('groups', 'dp'), ('expert', 'head')), parts along dimension 0, may hold values from -6 to 6
- guidance: float32 [4], P(('groups', 'dp')), parts along dimension 0, may hold values from 1.5 to 3
- step_size: float32 [4], P(('groups', 'dp')), parts along dimension 0, may hold values from 0.1 to 0.5
Outputs:
- next_latent: float32 [4, 1024, 16], P(('groups', 'dp'), ('expert', 'head')), parts along dimension 0
The draws below stay inside these ranges and needn't reach their ends.
There are 2 independent parts, one for each index of `groups`. The reference program is written for one: setup_inputs(seed, part) draws one part's arguments, and reference() takes and returns one part's arrays. A program takes and returns all parts, laid end to end along the dimension named above; an argument that names none is the same for every part. Nothing has to cross between parts.
Inputs may be any that keep to these rules, and one draw needn't show every extreme that they name: `route_ids`: each token names 2 different experts. In each aligned block of 128 tokens of a latent (tokens 128 j to 128 (j + 1) - 1), no expert is named by more than 32 routes, a bound that some block reaches.
All inputs are finite; a program needn't handle non-finite values.
Results may differ from the reference program's by a relative error of at most 0.0065.
Values may be sent and summed in bfloat16 or wider, within the bound.
A program may use at most 192 MiB of HBM per device.

```python
import math
import jax
import jax.numpy as jnp
import numpy as np
from jax import lax

D = 1536
FF = 6144
EXPERTS = 16
TOP = 2
GH = 6
HD = 64
DG = 384
P_SIZE = 16
SEQ = 1024
LATENTS = 2
TH = 128
CAP = 32
HIDDEN_SIZE = 98304
HS = 6144


def shard_levels(key, shape, cuts, smallest, high):
    level, own = 1.0, jax.random.fold_in(key, 6)
    for position, shards_of in cuts:
        steps = jnp.exp(jax.random.uniform(jax.random.fold_in(own, position), (shards_of,), jnp.float32, smallest / len(cuts), high / len(cuts)))
        level = level * jnp.repeat(steps, shape[position] // shards_of).reshape([-1 if axis == position else 1 for axis in range(len(shape))])
    return level


def routed_block(rng, own, number, rows, number_of, top, limit, slope):
    sequence = jax.random.permutation(rng, number_of)
    heavy_load, ordinary = portions_of(number_of, rows * top, limit, slope, True), portions_of(number_of, rows * top, limit, slope, False)
    places = jnp.arange(number_of)

    def named(tallies, turn):
        used = int((tallies > 0).sum())
        fixed = max(1, used // 4)
        shifted = fixed + (places - fixed + turn * (used - fixed)) % max(1, number_of - fixed)
        return jnp.zeros((number_of,), jnp.int32).at[sequence[jnp.where(places < fixed, places, shifted)]].set(jnp.asarray(tallies, jnp.int32))

    tallies = jnp.where(number % 4 == 0, named(heavy_load, number // 4), named(ordinary, number - number // 4 - 1))
    mixed = jax.random.permutation(jax.random.fold_in(own, 3), number_of)
    donor, taker = mixed[0:number_of // 2 * 2:2], mixed[1:number_of // 2 * 2:2]
    margin = jnp.minimum(tallies[donor] - 1, limit - tallies[taker]) // 2
    margin = jnp.where((donor == sequence[0]) | (taker == sequence[0]) | (tallies[taker] == 0), 0, jnp.maximum(margin, 0))
    shifted = jax.random.randint(jax.random.fold_in(own, 4), (number_of // 2,), 0, 1 << 20) % (margin + 1)
    tallies = tallies.at[donor].add(-shifted).at[taker].add(shifted)
    members = jnp.searchsorted(jnp.cumsum(tallies), jnp.arange(rows * top), side="right").astype(jnp.int32)
    table = members.reshape(top, rows).T
    table = table[jax.random.permutation(jax.random.fold_in(own, 1), rows)]
    turn = jax.random.randint(jax.random.fold_in(own, 2), (rows, 1), 0, top)
    return jnp.take_along_axis(table, (jnp.arange(top)[None, :] + turn) % top, axis=1)


def portions_of(count, total, limit, slope, full):
    portions = [(1 << 20) // math.isqrt(standing ** slope) + 1 for standing in range(1, count + 1)]
    largest = limit if full else min(limit, max(-(-total // count), total * portions[0] // sum(portions)))
    least = 1 if total - largest >= count - 1 else 0
    holding, surplus = [largest] + [least] * (count - 1), total - largest - least * (count - 1)
    while surplus > 0:
        free = [i for i in range(1, count) if holding[i] < largest] or [i for i in range(1, count) if holding[i] < limit]
        pool, remaining = sum([portions[i] for i in free]), surplus
        for i in free:
            more = min(limit - holding[i], max(1, remaining * portions[i] // pool), surplus)
            holding[i] = holding[i] + more
            surplus = surplus - more
    return np.array(holding)


def gaussian(key, shape, width, bound, cuts=(), kind=jnp.bfloat16):
    array = jax.random.normal(key, shape, jnp.float32) * width
    if len(cuts) > 0:
        array = shard_levels(key, shape, cuts, -0.22, 0.18) * array
    return jnp.clip(array, min=-bound, max=bound).astype(kind)


def setup_inputs(seed: int = 0, part: int = 0) -> dict:
    keys = jax.random.split(jax.random.key(seed), 15)
    own_keys = jax.random.split(jax.random.fold_in(keys[14], part), 15)
    hidden = gaussian(own_keys[0], (LATENTS, SEQ, D), 1.0, 6.0, ((0, 2), (1, 8)))
    modulation = gaussian(own_keys[1], (LATENTS, 3, D), 0.5, 3.0, ((0, 2),), jnp.float32)
    router_weight = gaussian(keys[2], (D, EXPERTS), D ** -0.5, 0.15625, (), jnp.float32)
    route_ids_keys = jax.random.split(jax.random.fold_in(own_keys[3], 1), LATENTS * SEQ // TH)
    route_ids_turns = jax.random.permutation(jax.random.fold_in(own_keys[3], 3), LATENTS * SEQ // TH)
    route_ids = jax.vmap(lambda own, number: routed_block(jax.random.fold_in(own_keys[3], 2), own, number, TH, EXPERTS, TOP, CAP, 2))(route_ids_keys, route_ids_turns).reshape((LATENTS, SEQ, TOP))
    gate_weight = gaussian(keys[4], (D, HIDDEN_SIZE), D ** -0.5, 0.15625, ((1, 16),))
    up_weight = gaussian(keys[5], (D, HIDDEN_SIZE), D ** -0.5, 0.15625, ((1, 16),))
    down_weight = gaussian(keys[6], (HIDDEN_SIZE, D), FF ** -0.5, 0.078125, ((0, 16),))
    main_final = gaussian(keys[7], (D, P_SIZE), D ** -0.5, 0.15625)
    guide_qkv = gaussian(own_keys[8], (LATENTS, SEQ, GH, 3 * HD), 1.0, 6.0, ((0, 2), (1, 4), (2, 2)))
    guide_out = gaussian(keys[9], (GH, HD, DG), DG ** -0.5, 0.3125, ((0, 2),))
    guide_final = gaussian(keys[10], (DG, P_SIZE), DG ** -0.5, 0.3125)
    latent = gaussian(own_keys[11], (LATENTS, SEQ, P_SIZE), 1.0, 6.0, ((0, 2), (1, 8)), jnp.float32)
    guidance = jnp.clip(1.5 + 1.5 * jax.random.uniform(own_keys[12], (LATENTS,), jnp.float32) ** shard_levels(own_keys[12], (LATENTS,), ((0, 2),), -0.2, 0.2), 1.5, 3.0)
    step_size = jnp.clip(0.1 + 0.4 * jax.random.uniform(own_keys[13], (LATENTS,), jnp.float32) ** shard_levels(own_keys[13], (LATENTS,), ((0, 2),), -0.2, 0.2), 0.1, 0.5)
    return dict(hidden=hidden, modulation=modulation, router_weight=router_weight, route_ids=route_ids, gate_weight=gate_weight, up_weight=up_weight, down_weight=down_weight, main_final=main_final, guide_qkv=guide_qkv, guide_out=guide_out, guide_final=guide_final, latent=latent, guidance=guidance, step_size=step_size)


epsilon = 1e-06
score_scale = 8.0

def layer_norm(values):
    average = lax.optimization_barrier(jnp.mean(values, axis=-1, keepdims=True))
    centered = values - average
    return centered / jnp.sqrt(lax.optimization_barrier(jnp.mean(centered * centered, axis=-1, keepdims=True)) + epsilon)

def unit_rows(values):
    return values / jnp.sqrt(lax.optimization_barrier(jnp.mean(values * values, axis=-1, keepdims=True)) + epsilon)

def reference(hidden, modulation, router_weight, route_ids, gate_weight, up_weight, down_weight, main_final, guide_qkv, guide_out, guide_final, latent, guidance, step_size):
    hidden_float = hidden.astype(jnp.float32)
    shift_rows = modulation[:, 0][:, None, :]
    scale_rows = modulation[:, 1][:, None, :]
    gate_rows = modulation[:, 2][:, None, :]
    modulated = (layer_norm(hidden_float) * (1.0 + scale_rows) + shift_rows).astype(jnp.bfloat16)
    token_total = LATENTS * SEQ
    flat_rows = modulated.reshape(token_total, D)
    logits = jnp.dot(flat_rows.astype(jnp.float32), router_weight, precision=lax.Precision.HIGHEST)
    flat_ids = route_ids.reshape(token_total, TOP).astype(jnp.int32)
    picked = jnp.take_along_axis(logits, flat_ids, axis=1)
    first_weight = jax.nn.sigmoid(picked[:, 0] - picked[:, 1])
    route_weight = jnp.stack([first_weight, 1.0 - first_weight], axis=1)
    route_total = token_total * TOP
    route_flat = flat_ids.reshape(route_total)
    row_limit = min(route_total, token_total // TH * CAP)
    block_count = FF // HS

    def one_expert(expert):
        not_mine = (route_flat != expert).astype(jnp.int32)
        order = jnp.argsort(not_mine, stable=True)[:row_limit].astype(jnp.int32)
        valid = (route_flat[order] == expert).astype(jnp.float32)[:, None]
        rows = flat_rows[order // TOP]
        start_unit = expert * FF
        gate_part = lax.dynamic_slice_in_dim(gate_weight, start_unit, FF, 1)
        up_part = lax.dynamic_slice_in_dim(up_weight, start_unit, FF, 1)
        down_part = lax.dynamic_slice_in_dim(down_weight, start_unit, FF, 0)
        gate_vals = jnp.dot(rows, gate_part, preferred_element_type=jnp.float32)
        up_vals = jnp.dot(rows, up_part, preferred_element_type=jnp.float32)
        activated = (jax.nn.silu(gate_vals) * up_vals).astype(jnp.bfloat16)
        blocks = jnp.einsum('rbh,bhd->brd', activated.reshape(row_limit, block_count, HS).astype(jnp.float32), down_part.reshape(block_count, HS, D).astype(jnp.float32))
        rounded = lax.optimization_barrier(blocks.astype(jnp.bfloat16))
        return (lax.optimization_barrier(jnp.sum(rounded.astype(jnp.float32), axis=0)) * valid, order)
    results, orders = lax.map(one_expert, jnp.arange(EXPERTS, dtype=jnp.int32))
    per_route = jnp.zeros((route_total, D), jnp.float32).at[orders.reshape(-1)].add(results.reshape(-1, D))
    moe_out = lax.optimization_barrier(jnp.sum(per_route.reshape(token_total, TOP, D) * route_weight[:, :, None], axis=1))
    updated = hidden_float + gate_rows * moe_out.reshape(LATENTS, SEQ, D)
    main_norm = layer_norm(updated).astype(jnp.bfloat16)
    main_velocity = jnp.dot(main_norm.reshape(token_total, D), main_final, preferred_element_type=jnp.float32).reshape(LATENTS, SEQ, P_SIZE)
    queries = unit_rows(guide_qkv[..., :HD].astype(jnp.float32)).astype(jnp.bfloat16)
    unit_keys = unit_rows(guide_qkv[..., HD:2 * HD].astype(jnp.float32)).astype(jnp.bfloat16)
    values_part = guide_qkv[..., 2 * HD:]

    def one_latent(items):
        query_rows, key_rows, value_rows = items
        scores = jnp.einsum('qhc,khc->hqk', query_rows.astype(jnp.float32), key_rows.astype(jnp.float32)) * (score_scale / HD)
        weights = jnp.exp(scores - score_scale)
        totals = lax.optimization_barrier(jnp.sum(weights, axis=-1))
        rounded = lax.optimization_barrier(weights.astype(jnp.bfloat16))
        mixed = jnp.einsum('hqk,khc->qhc', rounded.astype(jnp.float32), value_rows.astype(jnp.float32))
        return (mixed / jnp.transpose(totals)[:, :, None]).astype(jnp.bfloat16)
    attended = lax.map(one_latent, (queries, unit_keys, values_part))
    guide_mix = jnp.einsum('lqhc,hcd->lqd', attended.astype(jnp.float32), guide_out.astype(jnp.float32))
    guide_norm = layer_norm(guide_mix).astype(jnp.bfloat16)
    guide_velocity = jnp.dot(guide_norm.reshape(token_total, DG), guide_final, preferred_element_type=jnp.float32).reshape(LATENTS, SEQ, P_SIZE)
    guided = guide_velocity + guidance[:, None, None] * (main_velocity - guide_velocity)
    return latent + step_size[:, None, None] * guided
```

```python
import functools

import jax
import jax.numpy as jnp
from jax import lax
from jax.experimental import pallas as pl
from jax.experimental.pallas import tpu as pltpu
from jax.sharding import PartitionSpec as P

FF = 6144
EXPERTS = 16
TOP = 2
HD = 64
P_SIZE = 16


epsilon = 1e-06
score_scale = 8.0


def layer_norm(values):
    average = jnp.mean(values, axis=-1, keepdims=True)
    centered = values - average
    return centered / jnp.sqrt(jnp.mean(centered * centered, axis=-1, keepdims=True) + epsilon)


def unit_rows(values):
    return values / jnp.sqrt(jnp.mean(values * values, axis=-1, keepdims=True) + epsilon)


def route_slots(flat_ids, block_slots, per_index, copies):
    route_flat = flat_ids.reshape(-1)
    one_hot = (route_flat[:, None] == jnp.arange(EXPERTS, dtype=jnp.int32)[None, :]).astype(
        jnp.int32
    )
    order = jnp.arange(route_flat.shape[0], dtype=jnp.int32)
    before = (order[None, :] < order[:, None]).astype(jnp.bfloat16)
    earlier = jnp.dot(before, one_hot.astype(jnp.bfloat16), preferred_element_type=jnp.float32)
    earlier_count = jnp.sum(earlier.astype(jnp.int32) * one_hot, axis=1)
    slot_pos = route_flat % per_index * block_slots + earlier_count
    targets = (
        route_flat[:, None] * copies + jnp.arange(copies, dtype=jnp.int32)[None, :]
    ) // per_index
    return (targets, slot_pos)


def expert_hidden(
    rows, positions, gate_weight, up_weight, my_expert, index_first, block_slots, copies
):
    owner_expert = (index_first + positions // block_slots) // copies
    keep_mask = (owner_expert == my_expert).astype(jnp.float32)[:, None]
    gate_vals = jnp.dot(rows, gate_weight, preferred_element_type=jnp.float32)
    up_vals = jnp.dot(rows, up_weight, preferred_element_type=jnp.float32)
    return (jax.nn.silu(gate_vals) * up_vals * keep_mask).astype(jnp.bfloat16)


def plain_body(
    hidden,
    modulation,
    router_weight,
    route_ids,
    gate_weight,
    up_weight,
    down_weight,
    main_final,
    guide_qkv,
    guide_out,
    guide_final,
    latent,
    guidance,
    step_size,
):
    lat_dev, tok_dev, width = hidden.shape
    experts_axis = lax.axis_size("expert")
    group_size = lax.axis_size(("dp", "head"))
    slice_units = gate_weight.shape[1]
    index_units = slice_units * group_size
    if EXPERTS >= experts_axis:
        per_index = EXPERTS // experts_axis
        copies = 1
    else:
        per_index = 1
        copies = experts_axis // EXPERTS
    capacity = max(2, 2 * tok_dev * TOP // EXPERTS)
    block_slots = lat_dev * capacity
    slot_count = per_index * block_slots
    my_index = lax.axis_index("expert")
    my_member = lax.axis_index(("dp", "head"))
    my_expert = (my_index * index_units + my_member * slice_units) // FF
    index_first = my_index * per_index
    hidden_float = hidden.astype(jnp.float32)
    modulated = (
        layer_norm(hidden_float) * (1.0 + modulation[:, 1][:, None, :])
        + modulation[:, 0][:, None, :]
    ).astype(jnp.bfloat16)
    row_count = lat_dev * tok_dev
    flat_rows = modulated.reshape(row_count, width)
    logits = jnp.dot(flat_rows.astype(jnp.float32), router_weight, precision=lax.Precision.HIGHEST)
    flat_ids = route_ids.reshape(row_count, TOP)
    picked = jnp.take_along_axis(logits, flat_ids, axis=1)
    first_weight = jax.nn.sigmoid(picked[:, 0] - picked[:, 1])
    route_weight = jnp.stack([first_weight, 1.0 - first_weight], axis=1)
    targets, slot_pos = route_slots(flat_ids, block_slots, per_index, copies)
    flat_place = (targets * slot_count + slot_pos[:, None]).reshape(row_count, TOP * copies)
    all_places = jnp.arange(experts_axis * slot_count, dtype=jnp.int32)
    chosen = jnp.any(all_places[:, None, None] == flat_place[None], axis=2).astype(jnp.bfloat16)
    outgoing = jnp.dot(chosen, flat_rows, preferred_element_type=jnp.float32)
    outgoing = outgoing.astype(jnp.bfloat16).reshape(experts_axis, slot_count, width)
    received = lax.all_to_all(outgoing, "expert", split_axis=0, concat_axis=0, tiled=True)
    received_rows = received.reshape(experts_axis * slot_count, width)
    piece = lax.all_gather(received_rows, ("dp", "head"), axis=0, tiled=True)
    positions = jnp.arange(piece.shape[0], dtype=jnp.int32) % slot_count
    activated = expert_hidden(
        piece, positions, gate_weight, up_weight, my_expert, index_first, block_slots, copies
    )
    term = jnp.dot(activated, down_weight, preferred_element_type=jnp.float32)
    row_sums = lax.psum_scatter(
        lax.optimization_barrier(term.astype(jnp.bfloat16))
        .astype(jnp.float32)
        .astype(jnp.bfloat16),
        ("dp", "head"),
        scatter_dimension=0,
        tiled=True,
    ).astype(jnp.float32)
    returned = lax.all_to_all(
        row_sums.reshape(experts_axis, slot_count, width).astype(jnp.bfloat16),
        "expert",
        split_axis=0,
        concat_axis=0,
        tiled=True,
    ).astype(jnp.float32)
    gathered_back = returned[targets, slot_pos[:, None]]
    per_route = jnp.sum(gathered_back, axis=1).reshape(row_count, TOP, width)
    moe_out = jnp.sum(per_route * route_weight[:, :, None], axis=1)
    updated = hidden_float + modulation[:, 2][:, None, :] * moe_out.reshape(lat_dev, tok_dev, width)
    main_norm = layer_norm(updated).astype(jnp.bfloat16)
    main_velocity = jnp.dot(
        main_norm.reshape(row_count, width), main_final, preferred_element_type=jnp.float32
    ).reshape(lat_dev, tok_dev, P_SIZE)
    queries = unit_rows(guide_qkv[..., :HD].astype(jnp.float32)).astype(jnp.bfloat16)
    unit_keys = unit_rows(guide_qkv[..., HD : 2 * HD].astype(jnp.float32)).astype(jnp.bfloat16)
    key_value = jnp.concatenate([unit_keys, guide_qkv[..., 2 * HD :]], axis=-1)
    piece = lax.all_gather(key_value, "expert", axis=1, tiled=True)
    key_piece = piece[..., :HD]
    value_piece = piece[..., HD:]
    scores = jnp.einsum(
        "lqhc,lkhc->lhqk", queries, key_piece, preferred_element_type=jnp.float32
    ) * (score_scale / HD)
    weights = jnp.exp(scores - score_scale)
    weighted_sum = jnp.einsum(
        "lhqk,lkhc->lqhc",
        weights.astype(jnp.bfloat16),
        value_piece,
        preferred_element_type=jnp.float32,
    )
    weight_total = jnp.transpose(jnp.sum(weights, axis=-1), (0, 2, 1))
    weighted_sum, weight_total = (weighted_sum, weight_total)
    attended = (weighted_sum / weight_total[..., None]).astype(jnp.bfloat16)
    partial_mix = jnp.einsum(
        "lqhc,hcd->lqd", attended, guide_out, preferred_element_type=jnp.float32
    )
    guide_mix = lax.psum_scatter(
        partial_mix.astype(jnp.bfloat16), "head", scatter_dimension=1, tiled=True
    ).astype(jnp.float32)
    guide_norm = layer_norm(guide_mix).astype(jnp.bfloat16)
    guide_width = guide_norm.shape[-1]
    guide_velocity = jnp.dot(
        guide_norm.reshape(row_count, guide_width), guide_final, preferred_element_type=jnp.float32
    ).reshape(lat_dev, tok_dev, P_SIZE)
    guided = guide_velocity + guidance[:, None, None] * (main_velocity - guide_velocity)
    return latent + step_size[:, None, None] * guided


WEIGHT_SLOTS = 3
MESH = pl.DeviceIdType.MESH


def flipped(value, mask, bits):
    total = 0
    for bit in range(bits):
        digit = lax.rem(lax.div(value, jnp.int32(2**bit)), jnp.int32(2))
        if (mask >> bit) & 1:
            digit = 1 - digit
        total = total + digit * 2**bit
    return total


def slot_mask(slot):
    return (slot & 3) | ((slot & 4) << 1) | ((slot & 8) >> 1)


def fused_kernel(
    cap,
    tile,
    hidden_ref,
    modulation_ref,
    router_ref,
    ids_ref,
    slots_ref,
    slots_t_ref,
    qkv_ref,
    guide_out_ref,
    main_final_ref,
    guide_final_ref,
    latent_ref,
    guidance_ref,
    step_ref,
    gate_hbm,
    up_hbm,
    down_hbm,
    out_ref,
    outgoing,
    recv,
    result,
    back,
    total,
    kv,
    mix_own,
    mix_send,
    mix_recv,
    gate_buf,
    up_buf,
    down_buf,
    weight_sem,
    go_send,
    go_recv,
    back_send,
    back_recv,
    kv_send,
    kv_recv,
    pair_send,
    pair_recv,
):
    f32, bf16 = jnp.float32, jnp.bfloat16
    tokens, width = hidden_ref.shape
    heads, queries_dev, _ = qkv_ref.shape
    units = gate_hbm.shape[1]
    tiles = units // tile
    half = EXPERTS // 2
    half_rows = half * cap
    my_z, my_x, my_core = lax.axis_index("expert"), lax.axis_index("dp"), lax.axis_index("head")

    def device(mask):
        return {
            "expert": flipped(my_z, mask >> 2, 2),
            "dp": flipped(my_x, (mask >> 1) & 1, 1),
            "head": flipped(my_core, mask & 1, 1),
        }

    barrier = pltpu.get_barrier_semaphore()
    for mask in range(1, EXPERTS):
        pl.semaphore_signal(barrier, inc=1, device_id=device(mask), device_id_type=MESH)

    def weight_copies(step):
        slot = lax.rem(step, jnp.int32(WEIGHT_SLOTS))
        start = pl.multiple_of(lax.rem(step, jnp.int32(tiles)) * tile, tile)
        cols = pl.ds(start, tile)
        return (
            pltpu.make_async_copy(gate_hbm.at[:, cols], gate_buf.at[slot], weight_sem.at[0, slot]),
            pltpu.make_async_copy(up_hbm.at[:, cols], up_buf.at[slot], weight_sem.at[1, slot]),
            pltpu.make_async_copy(down_hbm.at[cols, :], down_buf.at[slot], weight_sem.at[2, slot]),
        )

    for step in range(WEIGHT_SLOTS - 1):
        for copy in weight_copies(jnp.int32(step)):
            copy.start()

    for h in range(heads):
        keys = unit_rows(qkv_ref[h, :, HD : 2 * HD].astype(f32)).astype(bf16)
        kv[0, h] = jnp.concatenate([keys, qkv_ref[h, :, 2 * HD :]], axis=-1)

    hidden_float = hidden_ref[...].astype(f32)
    modulated = (
        layer_norm(hidden_float) * (1.0 + modulation_ref[1:2, :]) + modulation_ref[0:1, :]
    ).astype(bf16)

    slot_row = slots_t_ref[...]
    kind = lax.broadcasted_iota(jnp.int32, (EXPERTS, tokens), 0)
    first_t = kind == slot_row[0:1, :]
    second_t = kind == slot_row[1:2, :]
    named_t = jnp.where(first_t | second_t, 1.0, 0.0).astype(bf16)
    row = lax.broadcasted_iota(jnp.int32, (tokens, tokens), 0)
    col = lax.broadcasted_iota(jnp.int32, (tokens, tokens), 1)
    earlier_t = jnp.dot(
        named_t, jnp.where(row < col, 1.0, 0.0).astype(bf16), preferred_element_type=f32
    )
    place_t = [
        slot_row[k : k + 1, :] * cap
        + jnp.sum(jnp.where(hot, earlier_t, 0.0), axis=0, keepdims=True).astype(jnp.int32)
        for k, hot in enumerate((first_t, second_t))
    ]
    for part in range(2):
        place = lax.broadcasted_iota(jnp.int32, (half_rows, tokens), 0) + part * half_rows
        chosen = jnp.where((place == place_t[0]) | (place == place_t[1]), 1.0, 0.0).astype(bf16)
        rows = jnp.dot(chosen, modulated, preferred_element_type=f32).astype(bf16)
        outgoing[pl.ds(part * half_rows, half_rows), :] = rows
        if part == 0:
            recv[pl.ds(0, cap), :] = rows[:cap]

    pl.semaphore_wait(barrier, EXPERTS - 1)

    kv_copies = []
    for j in range(1, kv.shape[0]):
        kv_copies.append(
            pltpu.make_async_remote_copy(
                src_ref=kv.at[0],
                dst_ref=kv.at[j],
                send_sem=kv_send.at[j],
                recv_sem=kv_recv.at[j],
                device_id=device(j << 2),
                device_id_type=MESH,
            )
        )
        kv_copies[-1].start()

    def row_copy(source, target, send_sem, recv_sem, slot):
        rows = pl.ds(slot * cap, cap)
        return pltpu.make_async_remote_copy(
            src_ref=source.at[rows, :],
            dst_ref=target.at[rows, :],
            send_sem=send_sem.at[slot],
            recv_sem=recv_sem.at[slot],
            device_id=device(slot_mask(slot)),
            device_id_type=MESH,
        )

    order = [[4, 5, 6, 7, 1, 2, 3], [12, 13, 14, 15, 8, 9, 10, 11]]
    go, home = {}, {}
    for part in range(2):
        for slot in order[part]:
            go[slot] = row_copy(outgoing, recv, go_send, go_recv, slot)
            go[slot].start()

    logits = jnp.dot(
        modulated.astype(f32), router_ref[...], precision=lax.Precision.HIGHEST,
        preferred_element_type=f32,
    )
    lane = lax.broadcasted_iota(jnp.int32, (tokens, EXPERTS), 1)
    ids = ids_ref[...]
    picked = [
        jnp.sum(jnp.where(lane == ids[:, k : k + 1], logits, 0.0), axis=1, keepdims=True)
        for k in range(TOP)
    ]
    first_weight = 1.0 / (1.0 + jnp.exp(picked[1] - picked[0]))
    route_weight = [first_weight, 1.0 - first_weight]
    slots = slots_ref[...]
    hot = [lane == slots[:, k : k + 1] for k in range(TOP)]
    earlier = jnp.dot(
        jnp.where(col < row, 1.0, 0.0).astype(bf16),
        jnp.where(hot[0] | hot[1], 1.0, 0.0).astype(bf16),
        preferred_element_type=f32,
    )
    places = [
        slots[:, k : k + 1] * cap
        + jnp.sum(jnp.where(hot[k], earlier, 0.0), axis=1, keepdims=True).astype(jnp.int32)
        for k in range(TOP)
    ]

    for copy in kv_copies:
        copy.wait_recv()
    mix = jnp.zeros((queries_dev, guide_out_ref.shape[-1]), f32)
    for h in range(heads):
        queries = unit_rows(qkv_ref[h, :, :HD].astype(f32)).astype(bf16)
        weight_total = jnp.zeros((queries_dev, 1), f32)
        weighted = jnp.zeros((queries_dev, HD), f32)
        for j in range(kv.shape[0]):
            scores = lax.dot_general(
                queries, kv[j, h, :, :HD], (((1,), (1,)), ((), ())), preferred_element_type=f32
            ) * (score_scale / HD)
            weights = jnp.exp(scores - score_scale)
            weight_total = weight_total + jnp.sum(weights, axis=-1, keepdims=True)
            weighted = weighted + jnp.dot(
                weights.astype(bf16), kv[j, h, :, HD:], preferred_element_type=f32
            )
        attended = (weighted / weight_total).astype(bf16)
        mix = mix + jnp.dot(attended, guide_out_ref[h], preferred_element_type=f32)
    mix = mix.reshape(2, tokens, mix.shape[-1])
    mix_own[...] = mix
    mix_send[...] = mix.astype(bf16)
    pair = pltpu.make_async_remote_copy(
        src_ref=mix_send.at[1 - my_core],
        dst_ref=mix_recv,
        send_sem=pair_send,
        recv_sem=pair_recv,
        device_id=device(1),
        device_id_type=MESH,
    )
    pair.start()

    for part in range(2):
        for slot in order[part]:
            go[slot].wait_recv()
        total[...] = jnp.zeros_like(total)

        def expert_step(t, carry, part=part):
            step = t + part * tiles
            slot = lax.rem(step, jnp.int32(WEIGHT_SLOTS))

            @pl.when(step + (WEIGHT_SLOTS - 1) < 2 * tiles)
            def _():
                for copy in weight_copies(step + (WEIGHT_SLOTS - 1)):
                    copy.start()

            for copy in weight_copies(step):
                copy.wait()
            rows = recv[pl.ds(part * half_rows, half_rows), :]
            gate_vals = jnp.dot(rows, gate_buf[slot], preferred_element_type=f32)
            up_vals = jnp.dot(rows, up_buf[slot], preferred_element_type=f32)
            activated = (gate_vals / (1.0 + jnp.exp(-gate_vals)) * up_vals).astype(bf16)
            total[...] += jnp.dot(activated, down_buf[slot], preferred_element_type=f32)
            return carry

        lax.fori_loop(jnp.int32(0), jnp.int32(tiles), expert_step, jnp.int32(0))
        result[pl.ds(part * half_rows, half_rows), :] = total[...].astype(bf16)
        for slot in order[part]:
            home[slot] = row_copy(result, back, back_send, back_recv, slot)
            home[slot].start()
        if part == 0:
            back[pl.ds(0, cap), :] = result[pl.ds(0, cap), :]

    pair.wait_recv()
    guide_norm = layer_norm(mix_own[my_core] + mix_recv[...].astype(f32)).astype(bf16)
    guide_velocity = jnp.dot(guide_norm, guide_final_ref[...], preferred_element_type=f32)

    moe = jnp.zeros((tokens, width), f32)
    for part in range(2):
        for slot in order[part]:
            home[slot].wait_recv()
        returned = back[pl.ds(part * half_rows, half_rows), :]
        place = lax.broadcasted_iota(jnp.int32, (tokens, half_rows), 1) + part * half_rows
        for k in range(TOP):
            chosen = jnp.where(place == places[k], 1.0, 0.0).astype(bf16)
            moe = moe + route_weight[k] * jnp.dot(chosen, returned, preferred_element_type=f32)
    updated = hidden_ref[...].astype(f32) + modulation_ref[2:3, :] * moe
    main_norm = layer_norm(updated).astype(bf16)
    main_velocity = jnp.dot(main_norm, main_final_ref[...], preferred_element_type=f32)
    guided = guide_velocity + guidance_ref[...] * (main_velocity - guide_velocity)
    out_ref[...] = latent_ref[...] + step_ref[...] * guided

    for copy in kv_copies:
        copy.wait_send()
    for copies in (go, home):
        for slot in order[0] + order[1]:
            copies[slot].wait_send()
    pair.wait_send()


def fused_body(
    hidden,
    modulation,
    router_weight,
    route_ids,
    gate_weight,
    up_weight,
    down_weight,
    main_final,
    guide_qkv,
    guide_out,
    guide_final,
    latent,
    guidance,
    step_size,
):
    _, tokens, width = hidden.shape
    units = gate_weight.shape[1]
    cap = 2 * tokens * TOP // EXPERTS
    z_size = lax.axis_size("expert")
    tile = 512
    heads = guide_qkv.shape[2]
    queries_dev = guide_qkv.shape[1]
    guide_width = guide_out.shape[-1]
    ids = route_ids[0]
    slots = slot_mask(ids ^ lax.axis_index(("expert", "dp", "head")))
    qkv = jnp.transpose(guide_qkv[0], (1, 0, 2))
    vmem = pl.BlockSpec(memory_space=pltpu.VMEM)
    hbm = pl.BlockSpec(memory_space=pl.ANY)
    bf16, f32 = jnp.bfloat16, jnp.float32
    dma = pltpu.SemaphoreType.DMA
    row_total = EXPERTS * cap
    out = pl.pallas_call(
        functools.partial(fused_kernel, cap, tile),
        out_shape=jax.ShapeDtypeStruct((tokens, P_SIZE), f32),
        in_specs=[vmem] * 13 + [hbm] * 3,
        out_specs=vmem,
        scratch_shapes=[
            pltpu.VMEM((row_total, width), bf16),
            pltpu.VMEM((row_total, width), bf16),
            pltpu.VMEM((row_total, width), bf16),
            pltpu.VMEM((row_total, width), bf16),
            pltpu.VMEM((row_total // 2, width), f32),
            pltpu.VMEM((z_size, heads, queries_dev, 2 * HD), bf16),
            pltpu.VMEM((2, tokens, guide_width), f32),
            pltpu.VMEM((2, tokens, guide_width), bf16),
            pltpu.VMEM((tokens, guide_width), bf16),
            pltpu.VMEM((WEIGHT_SLOTS, width, tile), bf16),
            pltpu.VMEM((WEIGHT_SLOTS, width, tile), bf16),
            pltpu.VMEM((WEIGHT_SLOTS, tile, width), bf16),
            dma((3, WEIGHT_SLOTS)),
            dma((EXPERTS,)),
            dma((EXPERTS,)),
            dma((EXPERTS,)),
            dma((EXPERTS,)),
            dma((z_size,)),
            dma((z_size,)),
            dma,
            dma,
        ],
        compiler_params=pltpu.CompilerParams(
            collective_id=0, has_side_effects=True, vmem_limit_bytes=50 * 2**20
        ),
        cost_estimate=pl.CostEstimate(
            flops=6 * row_total * width * units,
            bytes_accessed=12 * width * units,
            transcendentals=row_total * units,
        ),
    )(
        hidden[0],
        modulation[0],
        router_weight,
        ids,
        slots,
        slots.T,
        qkv,
        guide_out,
        main_final,
        guide_final,
        latent[0],
        guidance[:, None],
        step_size[:, None],
        gate_weight,
        up_weight,
        down_weight,
    )
    return out[None]


def body(*arrays):
    hidden, gate_weight, guide_qkv = arrays[0], arrays[4], arrays[8]
    sizes = [lax.axis_size(name) for name in ("expert", "dp", "head")]
    whole_experts = gate_weight.shape[1] == FF and sizes == [4, 2, 2]
    if whole_experts and hidden.shape[0] == 1 and hidden.shape[1] % 128 == 0:
        return fused_body(*arrays)
    return plain_body(*arrays)


def solution(mesh):
    in_specs = (
        P(("groups", "dp"), ("expert", "head"), None),
        P(("groups", "dp"), None, None),
        P(),
        P(("groups", "dp"), ("expert", "head"), None),
        P(None, ("expert", "dp", "head")),
        P(None, ("expert", "dp", "head")),
        P(("expert", "dp", "head"), None),
        P(),
        P(("groups", "dp"), "expert", "head", None),
        P("head", None, None),
        P(),
        P(("groups", "dp"), ("expert", "head"), None),
        P(("groups", "dp")),
        P(("groups", "dp")),
    )
    out_specs = P(("groups", "dp"), ("expert", "head"), None)
    return jax.shard_map(body, mesh=mesh, in_specs=in_specs, out_specs=out_specs, check_vma=False)
```

```python
import functools

import jax
import jax.numpy as jnp
from jax import lax
from jax.experimental import pallas as pl
from jax.experimental.pallas import tpu as pltpu
from jax.sharding import PartitionSpec as P

FF = 6144
EXPERTS = 16
TOP = 2
HD = 64
P_SIZE = 16


epsilon = 1e-06
score_scale = 8.0


def layer_norm(values):
    average = jnp.mean(values, axis=-1, keepdims=True)
    centered = values - average
    return centered / jnp.sqrt(jnp.mean(centered * centered, axis=-1, keepdims=True) + epsilon)


def unit_rows(values):
    return values / jnp.sqrt(jnp.mean(values * values, axis=-1, keepdims=True) + epsilon)


def route_slots(flat_ids, block_slots, per_index, copies):
    route_flat = flat_ids.reshape(-1)
    one_hot = (route_flat[:, None] == jnp.arange(EXPERTS, dtype=jnp.int32)[None, :]).astype(
        jnp.int32
    )
    order = jnp.arange(route_flat.shape[0], dtype=jnp.int32)
    before = (order[None, :] < order[:, None]).astype(jnp.bfloat16)
    earlier = jnp.dot(before, one_hot.astype(jnp.bfloat16), preferred_element_type=jnp.float32)
    earlier_count = jnp.sum(earlier.astype(jnp.int32) * one_hot, axis=1)
    slot_pos = route_flat % per_index * block_slots + earlier_count
    targets = (
        route_flat[:, None] * copies + jnp.arange(copies, dtype=jnp.int32)[None, :]
    ) // per_index
    return (targets, slot_pos)


def expert_hidden(
    rows, positions, gate_weight, up_weight, my_expert, index_first, block_slots, copies
):
    owner_expert = (index_first + positions // block_slots) // copies
    keep_mask = (owner_expert == my_expert).astype(jnp.float32)[:, None]
    gate_vals = jnp.dot(rows, gate_weight, preferred_element_type=jnp.float32)
    up_vals = jnp.dot(rows, up_weight, preferred_element_type=jnp.float32)
    return (jax.nn.silu(gate_vals) * up_vals * keep_mask).astype(jnp.bfloat16)


def plain_body(
    hidden,
    modulation,
    router_weight,
    route_ids,
    gate_weight,
    up_weight,
    down_weight,
    main_final,
    guide_qkv,
    guide_out,
    guide_final,
    latent,
    guidance,
    step_size,
):
    lat_dev, tok_dev, width = hidden.shape
    experts_axis = lax.axis_size("expert")
    group_size = lax.axis_size(("dp", "head"))
    slice_units = gate_weight.shape[1]
    index_units = slice_units * group_size
    if EXPERTS >= experts_axis:
        per_index = EXPERTS // experts_axis
        copies = 1
    else:
        per_index = 1
        copies = experts_axis // EXPERTS
    capacity = max(2, 2 * tok_dev * TOP // EXPERTS)
    block_slots = lat_dev * capacity
    slot_count = per_index * block_slots
    my_index = lax.axis_index("expert")
    my_member = lax.axis_index(("dp", "head"))
    my_expert = (my_index * index_units + my_member * slice_units) // FF
    index_first = my_index * per_index
    hidden_float = hidden.astype(jnp.float32)
    modulated = (
        layer_norm(hidden_float) * (1.0 + modulation[:, 1][:, None, :])
        + modulation[:, 0][:, None, :]
    ).astype(jnp.bfloat16)
    row_count = lat_dev * tok_dev
    flat_rows = modulated.reshape(row_count, width)
    logits = jnp.dot(flat_rows.astype(jnp.float32), router_weight, precision=lax.Precision.HIGHEST)
    flat_ids = route_ids.reshape(row_count, TOP)
    picked = jnp.take_along_axis(logits, flat_ids, axis=1)
    first_weight = jax.nn.sigmoid(picked[:, 0] - picked[:, 1])
    route_weight = jnp.stack([first_weight, 1.0 - first_weight], axis=1)
    targets, slot_pos = route_slots(flat_ids, block_slots, per_index, copies)
    flat_place = (targets * slot_count + slot_pos[:, None]).reshape(row_count, TOP * copies)
    all_places = jnp.arange(experts_axis * slot_count, dtype=jnp.int32)
    chosen = jnp.any(all_places[:, None, None] == flat_place[None], axis=2).astype(jnp.bfloat16)
    outgoing = jnp.dot(chosen, flat_rows, preferred_element_type=jnp.float32)
    outgoing = outgoing.astype(jnp.bfloat16).reshape(experts_axis, slot_count, width)
    received = lax.all_to_all(outgoing, "expert", split_axis=0, concat_axis=0, tiled=True)
    received_rows = received.reshape(experts_axis * slot_count, width)
    piece = lax.all_gather(received_rows, ("dp", "head"), axis=0, tiled=True)
    positions = jnp.arange(piece.shape[0], dtype=jnp.int32) % slot_count
    activated = expert_hidden(
        piece, positions, gate_weight, up_weight, my_expert, index_first, block_slots, copies
    )
    term = jnp.dot(activated, down_weight, preferred_element_type=jnp.float32)
    row_sums = lax.psum_scatter(
        lax.optimization_barrier(term.astype(jnp.bfloat16))
        .astype(jnp.float32)
        .astype(jnp.bfloat16),
        ("dp", "head"),
        scatter_dimension=0,
        tiled=True,
    ).astype(jnp.float32)
    returned = lax.all_to_all(
        row_sums.reshape(experts_axis, slot_count, width).astype(jnp.bfloat16),
        "expert",
        split_axis=0,
        concat_axis=0,
        tiled=True,
    ).astype(jnp.float32)
    gathered_back = returned[targets, slot_pos[:, None]]
    per_route = jnp.sum(gathered_back, axis=1).reshape(row_count, TOP, width)
    moe_out = jnp.sum(per_route * route_weight[:, :, None], axis=1)
    updated = hidden_float + modulation[:, 2][:, None, :] * moe_out.reshape(lat_dev, tok_dev, width)
    main_norm = layer_norm(updated).astype(jnp.bfloat16)
    main_velocity = jnp.dot(
        main_norm.reshape(row_count, width), main_final, preferred_element_type=jnp.float32
    ).reshape(lat_dev, tok_dev, P_SIZE)
    queries = unit_rows(guide_qkv[..., :HD].astype(jnp.float32)).astype(jnp.bfloat16)
    unit_keys = unit_rows(guide_qkv[..., HD : 2 * HD].astype(jnp.float32)).astype(jnp.bfloat16)
    key_value = jnp.concatenate([unit_keys, guide_qkv[..., 2 * HD :]], axis=-1)
    piece = lax.all_gather(key_value, "expert", axis=1, tiled=True)
    key_piece = piece[..., :HD]
    value_piece = piece[..., HD:]
    scores = jnp.einsum(
        "lqhc,lkhc->lhqk", queries, key_piece, preferred_element_type=jnp.float32
    ) * (score_scale / HD)
    weights = jnp.exp(scores - score_scale)
    weighted_sum = jnp.einsum(
        "lhqk,lkhc->lqhc",
        weights.astype(jnp.bfloat16),
        value_piece,
        preferred_element_type=jnp.float32,
    )
    weight_total = jnp.transpose(jnp.sum(weights, axis=-1), (0, 2, 1))
    weighted_sum, weight_total = (weighted_sum, weight_total)
    attended = (weighted_sum / weight_total[..., None]).astype(jnp.bfloat16)
    partial_mix = jnp.einsum(
        "lqhc,hcd->lqd", attended, guide_out, preferred_element_type=jnp.float32
    )
    guide_mix = lax.psum_scatter(
        partial_mix.astype(jnp.bfloat16), "head", scatter_dimension=1, tiled=True
    ).astype(jnp.float32)
    guide_norm = layer_norm(guide_mix).astype(jnp.bfloat16)
    guide_width = guide_norm.shape[-1]
    guide_velocity = jnp.dot(
        guide_norm.reshape(row_count, guide_width), guide_final, preferred_element_type=jnp.float32
    ).reshape(lat_dev, tok_dev, P_SIZE)
    guided = guide_velocity + guidance[:, None, None] * (main_velocity - guide_velocity)
    return latent + step_size[:, None, None] * guided


WEIGHT_SLOTS = 3
MESH = pl.DeviceIdType.MESH


def flipped(value, mask, bits):
    total = 0
    for bit in range(bits):
        digit = lax.rem(lax.div(value, jnp.int32(2**bit)), jnp.int32(2))
        if (mask >> bit) & 1:
            digit = 1 - digit
        total = total + digit * 2**bit
    return total


def unit_columns(values):
    return values / jnp.sqrt(jnp.mean(values * values, axis=0, keepdims=True) + epsilon)


def slot_mask(slot):
    return (slot & 3) | ((slot & 4) << 1) | ((slot & 8) >> 1)


def fused_kernel(
    cap,
    tile,
    hidden_ref,
    modulation_ref,
    router_ref,
    ids_t_ref,
    slots_t_ref,
    qkv_ref,
    guide_out_ref,
    main_final_ref,
    guide_final_ref,
    latent_ref,
    guidance_ref,
    step_ref,
    gate_hbm,
    up_hbm,
    down_hbm,
    out_ref,
    outgoing,
    recv,
    result,
    back,
    total,
    kv,
    mix_own,
    mix_send,
    mix_recv,
    gate_buf,
    up_buf,
    down_buf,
    weight_sem,
    go_send,
    go_recv,
    back_send,
    back_recv,
    kv_send,
    kv_recv,
    pair_send,
    pair_recv,
):
    f32, bf16 = jnp.float32, jnp.bfloat16
    tokens, width = hidden_ref.shape
    heads, _, queries_dev = qkv_ref.shape
    units = gate_hbm.shape[1]
    tiles = units // tile
    half = EXPERTS // 2
    half_rows = half * cap
    my_z, my_x, my_core = lax.axis_index("expert"), lax.axis_index("dp"), lax.axis_index("head")

    def device(mask):
        return {
            "expert": flipped(my_z, mask >> 2, 2),
            "dp": flipped(my_x, (mask >> 1) & 1, 1),
            "head": flipped(my_core, mask & 1, 1),
        }

    barrier = pltpu.get_barrier_semaphore()
    for mask in range(1, EXPERTS):
        pl.semaphore_signal(barrier, inc=1, device_id=device(mask), device_id_type=MESH)

    def weight_copies(step):
        slot = lax.rem(step, jnp.int32(WEIGHT_SLOTS))
        start = pl.multiple_of(lax.rem(step, jnp.int32(tiles)) * tile, tile)
        cols = pl.ds(start, tile)
        return (
            pltpu.make_async_copy(gate_hbm.at[:, cols], gate_buf.at[slot], weight_sem.at[0, slot]),
            pltpu.make_async_copy(up_hbm.at[:, cols], up_buf.at[slot], weight_sem.at[1, slot]),
            pltpu.make_async_copy(down_hbm.at[cols, :], down_buf.at[slot], weight_sem.at[2, slot]),
        )

    for step in range(WEIGHT_SLOTS - 1):
        for copy in weight_copies(jnp.int32(step)):
            copy.start()

    for h in range(heads):
        kv[my_z, h, :HD] = unit_columns(qkv_ref[h, HD : 2 * HD].astype(f32)).astype(bf16)
        kv[my_z, h, HD:] = qkv_ref[h, 2 * HD :]

    hidden_float = hidden_ref[...].astype(f32)
    modulated = (
        layer_norm(hidden_float) * (1.0 + modulation_ref[1]) + modulation_ref[0]
    ).astype(bf16)

    slot_row = slots_t_ref[...]
    kind = lax.broadcasted_iota(jnp.int32, (EXPERTS, tokens), 0)
    first_t = kind == slot_row[0:1, :]
    second_t = kind == slot_row[1:2, :]
    named_t = jnp.where(first_t | second_t, 1.0, 0.0).astype(bf16)
    row = lax.broadcasted_iota(jnp.int32, (tokens, tokens), 0)
    col = lax.broadcasted_iota(jnp.int32, (tokens, tokens), 1)
    earlier_t = jnp.dot(
        named_t, jnp.where(row < col, 1.0, 0.0).astype(bf16), preferred_element_type=f32
    )
    place_t = [
        slot_row[k : k + 1, :] * cap
        + jnp.sum(jnp.where(hot, earlier_t, 0.0), axis=0, keepdims=True).astype(jnp.int32)
        for k, hot in enumerate((first_t, second_t))
    ]
    for part in range(2):
        place = lax.broadcasted_iota(jnp.int32, (half_rows, tokens), 0) + part * half_rows
        chosen = jnp.where((place == place_t[0]) | (place == place_t[1]), 1.0, 0.0).astype(bf16)
        rows = jnp.dot(chosen, modulated, preferred_element_type=f32).astype(bf16)
        outgoing[pl.ds(part * half_rows, half_rows), :] = rows
        if part == 0:
            recv[pl.ds(0, cap), :] = rows[:cap]

    pl.semaphore_wait(barrier, EXPERTS - 1)

    in_middle = jnp.logical_or(my_z == 1, my_z == 2)

    def kv_copy(owner_mask, target_mask, send, receive):
        block = flipped(my_z, owner_mask, 2)
        return pltpu.make_async_remote_copy(
            src_ref=kv.at[block],
            dst_ref=kv.at[block],
            send_sem=kv_send.at[send],
            recv_sem=kv_recv.at[receive],
            device_id=device(target_mask << 2),
            device_id_type=MESH,
        )

    kv_near = kv_copy(0, 1, 0, 0)
    kv_own_over = kv_copy(0, 3, 1, 1)
    kv_near_over = kv_copy(1, 3, 2, 2)
    kv_own_on = kv_copy(3, 1, 3, 1)
    kv_near_on = kv_copy(2, 1, 4, 2)
    kv_near.start()
    pl.when(in_middle)(kv_own_over.start)

    def row_copy(source, target, send_sem, recv_sem, slot):
        rows = pl.ds(slot * cap, cap)
        return pltpu.make_async_remote_copy(
            src_ref=source.at[rows, :],
            dst_ref=target.at[rows, :],
            send_sem=send_sem.at[slot],
            recv_sem=recv_sem.at[slot],
            device_id=device(slot_mask(slot)),
            device_id_type=MESH,
        )

    order = [[4, 5, 6, 7, 1, 2, 3], [12, 13, 14, 15, 8, 9, 10, 11]]
    go, home = {}, {}
    for part in range(2):
        for slot in order[part]:
            go[slot] = row_copy(outgoing, recv, go_send, go_recv, slot)
            go[slot].start()

    logits = lax.dot_general(
        router_ref[...],
        modulated.astype(f32),
        (((1,), (1,)), ((), ())),
        precision=lax.Precision.HIGHEST,
        preferred_element_type=f32,
    )
    ids_t = ids_t_ref[...]
    picked = [
        jnp.sum(jnp.where(kind == ids_t[k : k + 1, :], logits, 0.0), axis=0, keepdims=True)
        for k in range(TOP)
    ]

    def as_column(values):
        return jnp.sum(jnp.where(row == col, values, 0.0), axis=1, keepdims=True)

    first_weight = as_column(1.0 / (1.0 + jnp.exp(picked[1] - picked[0])))
    route_weight = [first_weight, 1.0 - first_weight]
    places = [as_column(place.astype(f32)).astype(jnp.int32) for place in place_t]

    kv_near.wait_recv()
    pl.when(in_middle)(kv_near_over.start)

    for part in range(2):
        for slot in order[part]:
            go[slot].wait_recv()
        total[...] = jnp.zeros_like(total)

        def expert_step(t, carry, part=part):
            step = t + part * tiles
            slot = lax.rem(step, jnp.int32(WEIGHT_SLOTS))

            @pl.when(step + (WEIGHT_SLOTS - 1) < 2 * tiles)
            def _():
                for copy in weight_copies(step + (WEIGHT_SLOTS - 1)):
                    copy.start()

            for copy in weight_copies(step):
                copy.wait()
            rows = recv[pl.ds(part * half_rows, half_rows), :]
            gate_vals = jnp.dot(rows, gate_buf[slot], preferred_element_type=f32)
            up_vals = jnp.dot(rows, up_buf[slot], preferred_element_type=f32)
            activated = (gate_vals / (1.0 + jnp.exp(-gate_vals)) * up_vals).astype(bf16)
            total[...] += jnp.dot(activated, down_buf[slot], preferred_element_type=f32)
            return carry

        lax.fori_loop(jnp.int32(0), jnp.int32(tiles), expert_step, jnp.int32(0))
        result[pl.ds(part * half_rows, half_rows), :] = total[...].astype(bf16)
        for slot in order[part]:
            home[slot] = row_copy(result, back, back_send, back_recv, slot)
            home[slot].start()
        if part == 0:
            back[pl.ds(0, cap), :] = result[pl.ds(0, cap), :]

            @pl.when(in_middle)
            def _():
                kv_own_over.wait_recv()
                kv_own_on.start()
                kv_near_over.wait_recv()
                kv_near_on.start()


    @pl.when(jnp.logical_not(in_middle))
    def _():
        kv_own_over.wait_recv()
        kv_near_over.wait_recv()

    mix = jnp.zeros((queries_dev, guide_out_ref.shape[-1]), f32)
    for h in range(heads):
        queries = unit_columns(qkv_ref[h, :HD].astype(f32)).astype(bf16)
        weight_total = jnp.zeros((1, queries_dev), f32)
        weighted = jnp.zeros((HD, queries_dev), f32)
        for j in range(kv.shape[0]):
            scores = lax.dot_general(
                kv[j, h, :HD], queries, (((0,), (0,)), ((), ())), preferred_element_type=f32
            ) * (score_scale / HD)
            weights = jnp.exp(scores - score_scale)
            weight_total = weight_total + jnp.sum(weights, axis=0, keepdims=True)
            weighted = weighted + jnp.dot(
                kv[j, h, HD:], weights.astype(bf16), preferred_element_type=f32
            )
        attended = (weighted / weight_total).astype(bf16)
        mix = mix + lax.dot_general(
            attended, guide_out_ref[h], (((0,), (0,)), ((), ())), preferred_element_type=f32
        )
    mix = mix.reshape(2, tokens, mix.shape[-1])
    mix_own[...] = mix
    mix_send[...] = mix.astype(bf16)
    pair = pltpu.make_async_remote_copy(
        src_ref=mix_send.at[1 - my_core],
        dst_ref=mix_recv,
        send_sem=pair_send,
        recv_sem=pair_recv,
        device_id=device(1),
        device_id_type=MESH,
    )
    pair.start()

    pair.wait_recv()
    guide_norm = layer_norm(mix_own[my_core] + mix_recv[...].astype(f32)).astype(bf16)
    guide_velocity = lax.dot_general(
        guide_final_ref[...], guide_norm, (((1,), (1,)), ((), ())), preferred_element_type=f32
    )

    moe = jnp.zeros((tokens, width), f32)
    for part in range(2):
        for slot in order[part]:
            home[slot].wait_recv()
        returned = back[pl.ds(part * half_rows, half_rows), :]
        place = lax.broadcasted_iota(jnp.int32, (tokens, half_rows), 1) + part * half_rows
        for k in range(TOP):
            chosen = jnp.where(place == places[k], 1.0, 0.0).astype(bf16)
            moe = moe + route_weight[k] * jnp.dot(chosen, returned, preferred_element_type=f32)
    updated = hidden_ref[...].astype(f32) + modulation_ref[2] * moe
    main_norm = layer_norm(updated).astype(bf16)
    main_velocity = lax.dot_general(
        main_final_ref[...], main_norm, (((1,), (1,)), ((), ())), preferred_element_type=f32
    )
    guided = guide_velocity + guidance_ref[...] * (main_velocity - guide_velocity)
    out_ref[...] = latent_ref[...] + step_ref[...] * guided

    kv_near.wait_send()

    @pl.when(in_middle)
    def _():
        for copy in (kv_own_over, kv_near_over, kv_own_on, kv_near_on):
            copy.wait_send()

    for copies in (go, home):
        for slot in order[0] + order[1]:
            copies[slot].wait_send()
    pair.wait_send()


def fused_body(
    hidden,
    modulation,
    router_weight,
    route_ids,
    gate_weight,
    up_weight,
    down_weight,
    main_final,
    guide_qkv,
    guide_out,
    guide_final,
    latent,
    guidance,
    step_size,
):
    _, tokens, width = hidden.shape
    units = gate_weight.shape[1]
    cap = 2 * tokens * TOP // EXPERTS
    z_size = lax.axis_size("expert")
    tile = 512
    heads = guide_qkv.shape[2]
    queries_dev = guide_qkv.shape[1]
    guide_width = guide_out.shape[-1]
    ids_t = route_ids[0].T
    slots_t = slot_mask(ids_t ^ lax.axis_index(("expert", "dp", "head")))
    qkv = jnp.transpose(guide_qkv[0], (1, 2, 0))
    vmem = pl.BlockSpec(memory_space=pltpu.VMEM)
    hbm = pl.BlockSpec(memory_space=pl.ANY)
    bf16, f32 = jnp.bfloat16, jnp.float32
    dma = pltpu.SemaphoreType.DMA
    row_total = EXPERTS * cap
    out = pl.pallas_call(
        functools.partial(fused_kernel, cap, tile),
        out_shape=jax.ShapeDtypeStruct((P_SIZE, tokens), f32),
        in_specs=[vmem] * 12 + [hbm] * 3,
        out_specs=vmem,
        scratch_shapes=[
            pltpu.VMEM((row_total, width), bf16),
            pltpu.VMEM((row_total, width), bf16),
            pltpu.VMEM((row_total, width), bf16),
            pltpu.VMEM((row_total, width), bf16),
            pltpu.VMEM((row_total // 2, width), f32),
            pltpu.VMEM((z_size, heads, 2 * HD, queries_dev), bf16),
            pltpu.VMEM((2, tokens, guide_width), f32),
            pltpu.VMEM((2, tokens, guide_width), bf16),
            pltpu.VMEM((tokens, guide_width), bf16),
            pltpu.VMEM((WEIGHT_SLOTS, width, tile), bf16),
            pltpu.VMEM((WEIGHT_SLOTS, width, tile), bf16),
            pltpu.VMEM((WEIGHT_SLOTS, tile, width), bf16),
            dma((3, WEIGHT_SLOTS)),
            dma((EXPERTS,)),
            dma((EXPERTS,)),
            dma((EXPERTS,)),
            dma((EXPERTS,)),
            dma((5,)),
            dma((3,)),
            dma,
            dma,
        ],
        compiler_params=pltpu.CompilerParams(
            collective_id=0, has_side_effects=True, vmem_limit_bytes=50 * 2**20
        ),
        cost_estimate=pl.CostEstimate(
            flops=6 * row_total * width * units,
            bytes_accessed=12 * width * units,
            transcendentals=row_total * units,
        ),
    )(
        hidden[0],
        jnp.transpose(modulation, (1, 0, 2)),
        router_weight.T,
        ids_t,
        slots_t,
        qkv,
        guide_out,
        main_final.T,
        guide_final.T,
        latent[0].T,
        guidance[:, None],
        step_size[:, None],
        gate_weight,
        up_weight,
        down_weight,
    )
    return out.T[None]


def body(*arrays):
    hidden, gate_weight, guide_qkv = arrays[0], arrays[4], arrays[8]
    sizes = [lax.axis_size(name) for name in ("expert", "dp", "head")]
    whole_experts = gate_weight.shape[1] == FF and sizes == [4, 2, 2]
    if whole_experts and hidden.shape[0] == 1 and hidden.shape[1] % 128 == 0:
        return fused_body(*arrays)
    return plain_body(*arrays)


def solution(mesh):
    in_specs = (
        P(("groups", "dp"), ("expert", "head"), None),
        P(("groups", "dp"), None, None),
        P(),
        P(("groups", "dp"), ("expert", "head"), None),
        P(None, ("expert", "dp", "head")),
        P(None, ("expert", "dp", "head")),
        P(("expert", "dp", "head"), None),
        P(),
        P(("groups", "dp"), "expert", "head", None),
        P("head", None, None),
        P(),
        P(("groups", "dp"), ("expert", "head"), None),
        P(("groups", "dp")),
        P(("groups", "dp")),
    )
    out_specs = P(("groups", "dp"), ("expert", "head"), None)
    return jax.shard_map(body, mesh=mesh, in_specs=in_specs, out_specs=out_specs, check_vma=False)
```
